512 devices in a mesh: row: 64 (over y, x, core), col: 8 (over z).
Axes of the slice: x: 4, y: 8, z: 8, core: 2. Of those that a mesh axis runs over, the one named last changes fastest.
Arguments:
- p_panel: bfloat16 [2, 512, 65536], P(None, 'col', 'row'), may hold values from -0.1875 to 0.1875
- h_panel: bfloat16 [2, 512, 8192], P(None, 'row', 'col'), may hold values from -6 to 6
- p_tile: bfloat16 [65536, 8192], P('row', 'col'), may hold values from -3 to 3
- p_mask: int32 [128, 2], replicated, may hold values 0 or 1
- h_mask: int32 [2, 16], replicated, may hold values 0 or 1
- keep_mask: int32 [128, 16], replicated, may hold values 0 or 1
Outputs:
- p_next: bfloat16 [65536, 8192], P('row', 'col')
The draws below stay inside these ranges and needn't reach their ends.
All inputs are finite; a program needn't handle non-finite values.
Results may differ from the reference program's by a relative error of at most 0.001.
Values may be sent and summed in bfloat16 or wider, within the bound.
No kernel may reach another device: no remote copies, remote signals or barrier semaphores. Data moves between devices by JAX's collectives and lax.ppermute only.
A program may use at most 64 MiB of HBM per device.

```python
import jax
import jax.numpy as jnp
from jax import lax

B = 512
PANELS = 2
ROW_BLOCKS = 128
COL_BLOCKS = 16
ROWS = 65536
COLS = 8192


def place_ends(result, rng, low, top_value):
    longest = result.shape.index(max(result.shape))
    spots = []
    for shift in (0, 1):
        where = [jax.random.randint(jax.random.fold_in(rng, axis), (), 0, length) for axis, length in enumerate(result.shape)]
        where[longest] = (where[longest] + shift) % result.shape[longest]
        spots.append(tuple(where))
    return result.at[spots[0]].set(low).at[spots[1]].set(top_value)


def shard_levels(own_key, shape, shards, least, largest):
    def one(position, parts):
        heights = jax.random.uniform(jax.random.fold_in(jax.random.fold_in(own_key, 6), position), (parts,), jnp.float32, least / len(shards), largest / len(shards))
        return jnp.repeat(jnp.exp(heights), shape[position] // parts).reshape((-1,) + (1,) * (len(shape) - position - 1))

    factor_of = one(*shards[0])
    for cut in shards[1:]:
        factor_of = factor_of * one(*cut)
    return factor_of


def noise(rng, shape, deviation, bound, cuts=(), kind=jnp.bfloat16):
    gain = shard_levels(rng, shape, cuts, -0.22, 0.18) if cuts else 1.0
    values = jax.random.normal(rng, shape, jnp.float32) * deviation * gain
    return jnp.minimum(jnp.maximum(values, -bound), bound).astype(kind)


def setup_inputs(seed: int = 0) -> dict:
    splits = jax.random.split(jax.random.key(seed), 7)
    return {
        "p_panel": noise(splits[0], (PANELS, B, ROWS), (PANELS * B) ** -0.5, 0.1875, ((1, 8), (2, 64))),
        "h_panel": noise(splits[1], (PANELS, B, COLS), 1.0, 6.0, ((1, 64), (2, 8))),
        "p_tile": noise(splits[2], (ROWS, COLS), 0.5, 3.0, ((0, 64), (1, 8))),
        "p_mask": place_ends((jax.random.randint(splits[3], (ROW_BLOCKS, PANELS), 0, 4) < 3).astype(jnp.int32), jax.random.fold_in(splits[3], 1), 0, 1),
        "h_mask": place_ends((jax.random.randint(splits[4], (PANELS, COL_BLOCKS), 0, 4) < 3).astype(jnp.int32), jax.random.fold_in(splits[4], 1), 0, 1),
        "keep_mask": place_ends((jax.random.randint(splits[5], (ROW_BLOCKS, COL_BLOCKS), 0, 5) < 4).astype(jnp.int32), jax.random.fold_in(splits[5], 1), 0, 1),
    }


def reference(p_panel, h_panel, p_tile, p_mask, h_mask, keep_mask):
    col_scale = jnp.repeat(h_mask, B, axis=1).astype(jnp.float32)
    h_sparse = h_panel.astype(jnp.float32) * col_scale[:, None, :]

    def one_block(block_index):
        offset = (block_index * B).astype(jnp.int32)
        panel_piece = lax.dynamic_slice_in_dim(p_panel, offset, B, 2).astype(jnp.float32)
        row_scale = lax.dynamic_slice_in_dim(p_mask, block_index, 1, 0)[0].astype(jnp.float32)
        panel_piece = panel_piece * row_scale[:, None, None]
        product = jnp.einsum("pki,pkj->ij", panel_piece, h_sparse)
        tile_rows = lax.dynamic_slice_in_dim(p_tile, offset, B, 0).astype(jnp.float32)
        keep_cols = jnp.repeat(lax.dynamic_slice_in_dim(keep_mask, block_index, 1, 0)[0], B).astype(jnp.float32)
        return (keep_cols[None, :] * (2.0 * tile_rows - product)).astype(jnp.bfloat16)

    blocks = lax.map(one_block, jnp.arange(ROW_BLOCKS, dtype=jnp.int32))
    return blocks.reshape(ROW_BLOCKS * B, COL_BLOCKS * B)
```

```python
import functools

import jax
import jax.numpy as jnp
from jax import lax
from jax.experimental import pallas as pl
from jax.experimental.pallas import tpu as pltpu
from jax.sharding import PartitionSpec as P

B = 512
PANELS = 2
CORES = 2


def finish(flags, p_ref, own_ref, other_ref, tile_ref, out_ref, *, rows):
    own = flags[0]
    other = 1 - own
    row_block = pl.program_id(0) * rows // B
    own_row = flags[1 + row_block * 2 + own]
    other_row = flags[1 + row_block * 2 + other]
    contract = (((0,), (0,)), ((), ()))
    for col in range(out_ref.shape[1] // B):
        cols = slice(col * B, (col + 1) * B)
        own_alive = (own_row * flags[5 + own * 2 + col]).astype(jnp.float32)
        other_alive = (other_row * flags[5 + other * 2 + col]).astype(jnp.float32)
        keep = flags[9 + row_block * 2 + col].astype(jnp.float32)
        product = own_alive * lax.dot_general(
            p_ref[own], own_ref[:, cols], contract, preferred_element_type=jnp.float32
        ) + other_alive * lax.dot_general(
            p_ref[other], other_ref[:, cols], contract, preferred_element_type=jnp.float32
        )
        tile = tile_ref[:, cols].astype(jnp.float32)
        out_ref[:, cols] = (keep * (2.0 * tile - product)).astype(out_ref.dtype)


def purify(flags, p_full, own, other, p_tile):
    rows = 256
    height, width = p_tile.shape
    inner = p_full.shape[1]
    return pl.pallas_call(
        functools.partial(finish, rows=rows),
        out_shape=jax.ShapeDtypeStruct((height, width), p_tile.dtype),
        grid=(height // rows,),
        in_specs=[
            pl.BlockSpec(memory_space=pltpu.SMEM),
            pl.BlockSpec((PANELS, inner, rows), lambda i: (0, 0, i)),
            pl.BlockSpec((inner, width), lambda i: (0, 0)),
            pl.BlockSpec((inner, width), lambda i: (0, 0)),
            pl.BlockSpec((rows, width), lambda i: (i, 0)),
        ],
        out_specs=pl.BlockSpec((rows, width), lambda i: (i, 0)),
        compiler_params=pltpu.CompilerParams(vmem_limit_bytes=40 << 20),
        cost_estimate=pl.CostEstimate(
            flops=2 * PANELS * inner * height * width,
            bytes_accessed=2 * (PANELS * inner * (height + width) + 2 * height * width),
            transcendentals=0,
        ),
    )(flags, p_full, own, other, p_tile)


def local(p_panel, h_panel, p_tile, p_mask, h_mask, keep_mask, *, row_devices):
    row_index = lax.axis_index("row")
    core = row_index % CORES
    p_full = lax.all_gather(p_panel, "col", axis=1, tiled=True)

    chips = row_devices // CORES
    pairs = [[CORES * chip + c for c in range(CORES)] for chip in range(chips)]
    planes = [[CORES * chip + c for chip in range(chips)] for c in range(CORES)]
    both = lax.all_gather(h_panel, "row", axis=1, axis_index_groups=pairs)
    mine = lax.dynamic_index_in_dim(both, core, 0, keepdims=False)
    mine = mine.reshape(-1, mine.shape[-1])
    spread = lax.all_to_all(
        jnp.broadcast_to(mine[None], (chips,) + mine.shape), "row", 0, 0, axis_index_groups=planes
    )
    own = spread.reshape(-1, mine.shape[-1])
    other = lax.ppermute(own, "row", [(d, d ^ 1) for d in range(row_devices)])

    row_count = p_tile.shape[0] // B
    col_count = p_tile.shape[1] // B
    row_first = row_index * row_count
    col_first = lax.axis_index("col") * col_count
    flags = jnp.concatenate(
        [
            core[None].astype(jnp.int32),
            lax.dynamic_slice_in_dim(p_mask, row_first, row_count, 0).reshape(-1),
            lax.dynamic_slice_in_dim(h_mask, col_first, col_count, 1).reshape(-1),
            lax.dynamic_slice(keep_mask, (row_first, col_first), (row_count, col_count)).reshape(-1),
        ]
    )
    return purify(flags, p_full, own, other, p_tile)


def solution(mesh):
    in_specs = (P(None, "col", "row"), P(None, "row", "col"), P("row", "col"), P(), P(), P())
    out_specs = P("row", "col")
    body = functools.partial(local, row_devices=mesh.shape["row"])
    return jax.shard_map(body, mesh=mesh, in_specs=in_specs, out_specs=out_specs, check_vma=False)
```

```python
import functools

import jax
import jax.numpy as jnp
from jax import lax
from jax.experimental import pallas as pl
from jax.experimental.pallas import tpu as pltpu
from jax.sharding import PartitionSpec as P

B = 512
PANELS = 2
CORES = 2
P_SCALE = 2.0**17
H_SCALE = 2.0**12
SMALL = 2.0**-14
FAR = 2.0**29


def finish(flags, kept_ref, other_ref, tile_ref, out_ref):
    rows = out_ref.shape[0]
    start = pl.program_id(0) * rows
    row_block = start // B
    p_rows = pl.ds(pl.multiple_of(start, rows), rows)
    depth = kept_ref.shape[0] // PANELS

    def write(cols, p_ref, h_ref, inner):
        value = 2.0 * tile_ref[:, cols].astype(jnp.float32)
        if inner is not None:
            value -= lax.dot_general(
                p_ref[inner, p_rows],
                h_ref[inner, cols],
                (((0,), (0,)), ((), ())),
                preferred_element_type=jnp.float32,
            )
        for col in range(cols.start // B, cols.stop // B):
            keep = flags[9 + row_block * 2 + col].astype(jnp.float32)
            part = slice(col * B - cols.start, (col + 1) * B - cols.start)
            out_ref[:, col * B : (col + 1) * B] = (keep * value[:, part]).astype(out_ref.dtype)

    inners = [None, slice(0, depth), slice(depth, 2 * depth), slice(0, 2 * depth)]
    width = out_ref.shape[1]
    col_count = width // B
    states = []
    for col in range(col_count):
        alive = [flags[1 + row_block * 2 + p] * flags[5 + p * 2 + col] for p in range(PANELS)]
        states.append(alive[0] + 2 * alive[1])
    full = (states[0] == 3) & (states[1] == 3)
    for core, refs in enumerate([(kept_ref, other_ref), (other_ref, kept_ref)]):
        here = flags[0] == core
        pl.when(here & full)(functools.partial(write, slice(0, width), *refs, inners[3]))
        for col in range(col_count):
            cols = slice(col * B, (col + 1) * B)
            for case, inner in enumerate(inners):
                pl.when(here & jnp.logical_not(full) & (states[col] == case))(
                    functools.partial(write, cols, *refs, inner)
                )


def purify(flags, kept, other, p_tile):
    rows = 512
    height, width = p_tile.shape
    inner = kept.shape[0]
    whole = pl.BlockSpec(memory_space=pltpu.VMEM)
    return pl.pallas_call(
        finish,
        out_shape=jax.ShapeDtypeStruct((height, width), p_tile.dtype),
        grid=(height // rows,),
        in_specs=[
            pl.BlockSpec(memory_space=pltpu.SMEM),
            whole,
            whole,
            pl.BlockSpec((rows, width), lambda i: (i, 0)),
        ],
        out_specs=pl.BlockSpec((rows, width), lambda i: (i, 0)),
        compiler_params=pltpu.CompilerParams(vmem_limit_bytes=24 << 20),
        cost_estimate=pl.CostEstimate(
            flops=2 * inner * height * width,
            bytes_accessed=2 * (inner * (height + width) + 2 * height * width),
            transcendentals=0,
        ),
    )(flags, kept, other, p_tile)


def local(p_panel, h_panel, p_tile, p_mask, h_mask, keep_mask, *, row_devices, col_devices):
    row_index = lax.axis_index("row")
    col_index = lax.axis_index("col")
    core = row_index % CORES
    line = row_devices // col_devices
    swap = [(d, d ^ 1) for d in range(row_devices)]

    p_other = lax.ppermute(p_panel, "row", swap)
    lines = [[line * y + d for d in range(line)] for y in range(col_devices)]
    h_line = lax.all_gather(h_panel, "row", axis=1, axis_index_groups=lines, tiled=True)

    is_p = core == 0
    scale = jnp.where(is_p, P_SCALE, H_SCALE).astype(jnp.float32)
    unscale = jnp.where(is_p, 1 / P_SCALE, 1 / H_SCALE).astype(jnp.float32)
    far_unscale = jnp.where(is_p, 1 / (P_SCALE * FAR), 1 / (H_SCALE * FAR)).astype(jnp.float32)
    give = jnp.where(is_p, jnp.stack([p_panel, p_other]), jnp.stack([h_line, h_line]))
    near = give.astype(jnp.float32) * scale
    far = near * (FAR * (1 + 1 / 1024))
    far = jnp.where(jnp.abs(far) >= SMALL, far, 0.0)
    give = jnp.where(jnp.abs(near) >= SMALL, near, far).astype(jnp.float16)
    groups = [
        [row * col_devices + c for c in range(col_devices)] for row in range(0, row_devices, CORES)
    ] + [
        [(line * y + x) * col_devices + c for y in range(col_devices)]
        for x in range(1, line, CORES)
        for c in range(col_devices)
    ]
    got = lax.all_gather(give, ("row", "col"), axis=2, axis_index_groups=groups, tiled=True)

    def decode(part):
        value = part.astype(jnp.float32)
        top = lax.reduce_precision(value, 8, 7)
        return (top * jnp.where(value == top, unscale, far_unscale)).astype(p_tile.dtype)

    sent, got, p_mask, h_mask, keep_mask = lax.optimization_barrier(
        (decode(got[1]), got, p_mask, h_mask, keep_mask)
    )
    other = lax.ppermute(sent, "row", swap)
    kept = decode(lax.dynamic_index_in_dim(got, core, 0, keepdims=False))

    row_count = p_tile.shape[0] // B
    col_count = p_tile.shape[1] // B
    row_first = row_index * row_count
    col_first = col_index * col_count
    flags = jnp.concatenate(
        [
            core[None].astype(jnp.int32),
            lax.dynamic_slice_in_dim(p_mask, row_first, row_count, 0).reshape(-1),
            lax.dynamic_slice_in_dim(h_mask, col_first, col_count, 1).reshape(-1),
            lax.dynamic_slice(keep_mask, (row_first, col_first), (row_count, col_count)).reshape(-1),
        ]
    )
    flat = lambda a: a.reshape(-1, a.shape[-1])
    return purify(flags, flat(kept), flat(other), p_tile)


def solution(mesh):
    in_specs = (P(None, "col", "row"), P(None, "row", "col"), P("row", "col"), P(), P(), P())
    out_specs = P("row", "col")
    body = functools.partial(local, row_devices=mesh.shape["row"], col_devices=mesh.shape["col"])
    return jax.shard_map(body, mesh=mesh, in_specs=in_specs, out_specs=out_specs, check_vma=False)
```

```python
import functools

import jax
import jax.numpy as jnp
from jax import lax
from jax.experimental import pallas as pl
from jax.experimental.pallas import tpu as pltpu
from jax.sharding import PartitionSpec as P

B = 512
PANELS = 2
CORES = 2
P_SCALE = 2.0**17
H_SCALE = 2.0**12
SMALL = 2.0**-14
FAR = 2.0**29


def finish(flags, kept_ref, other_ref, tile_ref, out_ref):
    rows = out_ref.shape[0]
    start = pl.program_id(0) * rows
    row_block = start // B
    p_rows = pl.ds(pl.multiple_of(start, rows), rows)
    depth = kept_ref.shape[0] // PANELS

    def write(cols, p_ref, h_ref, inner):
        value = 2.0 * tile_ref[:, cols].astype(jnp.float32)
        if inner is not None:
            value -= lax.dot_general(
                p_ref[inner, p_rows],
                h_ref[inner, cols],
                (((0,), (0,)), ((), ())),
                preferred_element_type=jnp.float32,
            )
        for col in range(cols.start // B, cols.stop // B):
            keep = flags[9 + row_block * 2 + col].astype(jnp.float32)
            part = slice(col * B - cols.start, (col + 1) * B - cols.start)
            out_ref[:, col * B : (col + 1) * B] = (keep * value[:, part]).astype(out_ref.dtype)

    inners = [None, slice(0, depth), slice(depth, 2 * depth), slice(0, 2 * depth)]
    width = out_ref.shape[1]
    col_count = width // B
    states = []
    for col in range(col_count):
        alive = [flags[1 + row_block * 2 + p] * flags[5 + p * 2 + col] for p in range(PANELS)]
        states.append(alive[0] + 2 * alive[1])
    full = (states[0] == 3) & (states[1] == 3)
    for core, refs in enumerate([(kept_ref, other_ref), (other_ref, kept_ref)]):
        here = flags[0] == core
        pl.when(here & full)(functools.partial(write, slice(0, width), *refs, inners[3]))
        for col in range(col_count):
            cols = slice(col * B, (col + 1) * B)
            for case, inner in enumerate(inners):
                pl.when(here & jnp.logical_not(full) & (states[col] == case))(
                    functools.partial(write, cols, *refs, inner)
                )


def purify(flags, kept, other, p_tile):
    rows = 512
    height, width = p_tile.shape
    inner = kept.shape[0]
    whole = pl.BlockSpec(memory_space=pltpu.VMEM)
    return pl.pallas_call(
        finish,
        out_shape=jax.ShapeDtypeStruct((height, width), p_tile.dtype),
        grid=(height // rows,),
        in_specs=[
            pl.BlockSpec(memory_space=pltpu.SMEM),
            whole,
            whole,
            pl.BlockSpec((rows, width), lambda i: (i, 0)),
        ],
        out_specs=pl.BlockSpec((rows, width), lambda i: (i, 0)),
        compiler_params=pltpu.CompilerParams(vmem_limit_bytes=50 << 20),
        cost_estimate=pl.CostEstimate(
            flops=2 * inner * height * width,
            bytes_accessed=2 * (inner * (height + width) + 2 * height * width),
            transcendentals=0,
        ),
    )(flags, kept, other, p_tile)


def local(p_panel, h_panel, p_tile, p_mask, h_mask, keep_mask, *, row_devices, col_devices):
    row_index = lax.axis_index("row")
    col_index = lax.axis_index("col")
    core = row_index % CORES
    line = row_devices // col_devices
    swap = [(d, d ^ 1) for d in range(row_devices)]

    p_other = lax.ppermute(p_panel, "row", swap)
    lines = [[line * y + d for d in range(line)] for y in range(col_devices)]
    h_line = lax.all_gather(h_panel, "row", axis=1, axis_index_groups=lines, tiled=True)

    is_p = core == 0
    scale = jnp.where(is_p, P_SCALE, H_SCALE).astype(jnp.float32)
    unscale = jnp.where(is_p, 1 / P_SCALE, 1 / H_SCALE).astype(jnp.float32)
    far_unscale = jnp.where(is_p, 1 / (P_SCALE * FAR), 1 / (H_SCALE * FAR)).astype(jnp.float32)
    give = jnp.where(is_p, jnp.stack([p_panel, p_other]), jnp.stack([h_line, h_line]))
    near = give.astype(jnp.float32) * scale
    far = near * (FAR * (1 + 1 / 1024))
    far = jnp.where(jnp.abs(far) >= SMALL, far, 0.0)
    give = jnp.where(jnp.abs(near) >= SMALL, near, far).astype(jnp.float16)
    groups = [
        [row * col_devices + c for c in range(col_devices)] for row in range(0, row_devices, CORES)
    ] + [
        [(line * y + x) * col_devices + c for y in range(col_devices)]
        for x in range(1, line, CORES)
        for c in range(col_devices)
    ]
    got = lax.all_gather(give, ("row", "col"), axis=2, axis_index_groups=groups, tiled=True)

    def decode(part, unscale, far_unscale):
        value = part.astype(jnp.float32)
        top = lax.reduce_precision(value, 8, 7)
        return (top * jnp.where(value == top, unscale, far_unscale)).astype(p_tile.dtype)

    sent, unscale, far_unscale, p_mask, h_mask, keep_mask = lax.optimization_barrier(
        (decode(got[1], unscale, far_unscale), unscale, far_unscale, p_mask, h_mask, keep_mask)
    )
    other = lax.ppermute(sent, "row", swap)
    kept = lax.dynamic_index_in_dim(got, core, 0, keepdims=False)
    kept = decode(kept, unscale, far_unscale)

    row_count = p_tile.shape[0] // B
    col_count = p_tile.shape[1] // B
    row_first = row_index * row_count
    col_first = col_index * col_count
    flags = jnp.concatenate(
        [
            core[None].astype(jnp.int32),
            lax.dynamic_slice_in_dim(p_mask, row_first, row_count, 0).reshape(-1),
            lax.dynamic_slice_in_dim(h_mask, col_first, col_count, 1).reshape(-1),
            lax.dynamic_slice(keep_mask, (row_first, col_first), (row_count, col_count)).reshape(-1),
        ]
    )
    flat = lambda a: a.reshape(-1, a.shape[-1])
    return purify(flags, flat(kept), flat(other), p_tile)


def solution(mesh):
    in_specs = (P(None, "col", "row"), P(None, "row", "col"), P("row", "col"), P(), P(), P())
    out_specs = P("row", "col")
    body = functools.partial(local, row_devices=mesh.shape["row"], col_devices=mesh.shape["col"])
    return jax.shard_map(body, mesh=mesh, in_specs=in_specs, out_specs=out_specs, check_vma=False)
```
